128 devices in a mesh: gx: 4 (over x), gy: 32 (over z, y, core).
Axes of the slice: x: 4, y: 4, z: 4, core: 2. Of those that a mesh axis runs over, the one named last changes fastest.
Arguments:
- particles: float32 [7, 1048576], P(None, ('gx', 'gy')), as said below
- pair_list: int32 [24576, 2], P(('gx', 'gy')), may hold values from 0 to 2047, as said below
- pair_count: int32 [128], P(('gx', 'gy')), may hold values from 144 to 192, as said below
Outputs:
- velocity: float32 [3, 1048576], P(None, ('gx', 'gy'))
- stretching: float32 [3, 1048576], P(None, ('gx', 'gy'))
The draws below stay inside these ranges and needn't reach their ends.
Inputs may be any that keep to these rules, and one draw needn't show every extreme that they name: `particles`: row 6 (core radius) is positive; rows 0 to 5 are real-valued. `pair_list`: each listed pair, live or not, names two different clusters; with owners oa = A // 16 and ob = B // 16: oa <= ob <= oa + 6, and the pair stands in the slots of device (oa + ob) // 2. `pair_count`: some device is full in every draw.
All inputs are finite; a program needn't handle non-finite values.
Results may differ from the reference program's by a relative error of at most 0.0003.
Values sent between devices are 32-bit elements; how exact they have to be, the bound alone decides.
No kernel may reach another device: no remote copies, remote signals or barrier semaphores. Data moves between devices by JAX's collectives and lax.ppermute only.
A program may use at most 64 MiB of HBM per device.

```python
import jax
import jax.numpy as jnp
from jax import lax

CLUSTER = 512
CLUS_DEV = 16
REACH = 3
PAIR_CAP = 192
RANKS = 128
CLUSTERS = 2048
PARTICLES = 1048576


def draw_particles(key, part):
    key = jax.random.fold_in(key, 1)
    keys = jax.random.split(key, 4)
    cluster = jnp.arange(CLUSTERS)
    centre = 0.35 * (cluster // CLUS_DEV).astype(jnp.float32) + 0.03 * (cluster % CLUS_DEV).astype(jnp.float32)
    noise = 0.3 * jax.random.normal(keys[0], (3, CLUSTERS, CLUSTER), jnp.float32)
    strength = 0.1 * jax.random.normal(keys[1], (3, CLUSTERS, CLUSTER), jnp.float32)
    scale = jnp.exp(jax.random.uniform(keys[2], (1, CLUSTERS, 1), jnp.float32, -1.204, 1.0986))
    core = jnp.exp(jax.random.uniform(keys[3], (1, CLUSTERS, CLUSTER), jnp.float32, -1.897, -0.799))
    position = noise + jnp.stack([centre, 0.0 * centre, 0.0 * centre])[:, :, None]
    whole = jnp.concatenate([position, strength * scale, core], 0)
    return whole.reshape(7, PARTICLES)


def draw_pair_list(key, part):
    key = jax.random.fold_in(key, 2)
    keys = jax.random.split(key, 5)
    count = RANKS * PAIR_CAP
    slot = jnp.arange(count, dtype=jnp.int32)
    owner = slot // PAIR_CAP
    near = jax.random.randint(keys[0], (count,), 0, REACH + 1)
    near = jnp.minimum(jnp.minimum(near, owner), RANKS - 1 - owner)
    extra = jax.random.randint(keys[1], (count,), 0, 2)
    far = jnp.minimum(jnp.minimum(near + extra, REACH), RANKS - 1 - owner)
    lower = owner - near
    upper = owner + far
    first_local = jax.random.randint(keys[2], (count,), 0, CLUS_DEV)
    offset = jax.random.randint(keys[3], (count,), 1, CLUS_DEV)
    other_local = jax.random.randint(keys[4], (count,), 0, CLUS_DEV)
    second_local = jnp.where(lower == upper, (first_local + offset) % CLUS_DEV, other_local)
    return jnp.stack([lower * CLUS_DEV + first_local, upper * CLUS_DEV + second_local], 1).astype(jnp.int32)


def draw_pair_count(key, part):
    key = jax.random.fold_in(key, 3)
    keys = jax.random.split(key, 2)
    short = jax.random.randint(keys[0], (RANKS,), 0, PAIR_CAP // 4 + 1)
    busiest = jax.random.randint(keys[1], (), 0, RANKS)
    counts = PAIR_CAP - short
    return jnp.where(jnp.arange(RANKS) == busiest, PAIR_CAP, counts).astype(jnp.int32)


def setup_inputs(seed: int = 0) -> dict:
    streams_of = jax.random.split(jax.random.key(seed), 4)
    particles = draw_particles(jax.random.fold_in(streams_of[3], 71), 0)
    pair_list = draw_pair_list(jax.random.fold_in(streams_of[3], 71), 0)
    pair_count = draw_pair_count(jax.random.fold_in(streams_of[3], 71), 0)
    return {"particles": particles, "pair_list": pair_list, "pair_count": pair_count}


inv_four_pi = 0.07957747154594767

def cross_list(left, right):
    return [left[1] * right[2] - left[2] * right[1], left[2] * right[0] - left[0] * right[2], left[0] * right[1] - left[1] * right[0]]

def interact(first, second):
    radial = [first[c][:, None] - second[c][None, :] for c in range(3)]
    spread = 0.5 * (first[6][:, None] ** 2 + second[6][None, :] ** 2)
    rho = radial[0] * radial[0] + radial[1] * radial[1] + radial[2] * radial[2] + spread
    inverse = lax.rsqrt(rho)
    kernel = inverse * inverse * inverse
    steep = 3.0 * kernel * inverse * inverse
    alpha_first = [first[3 + c][:, None] for c in range(3)]
    alpha_second = [second[3 + c][None, :] for c in range(3)]
    cross_second = cross_list(radial, alpha_second)
    cross_first = cross_list(radial, alpha_first)
    proj_first = alpha_first[0] * radial[0] + alpha_first[1] * radial[1] + alpha_first[2] * radial[2]
    proj_second = alpha_second[0] * radial[0] + alpha_second[1] * radial[1] + alpha_second[2] * radial[2]
    vel_first = [-inv_four_pi * lax.optimization_barrier(jnp.sum(kernel * cross_second[c], 1)) for c in range(3)]
    vel_second = [inv_four_pi * lax.optimization_barrier(jnp.sum(kernel * cross_first[c], 0)) for c in range(3)]
    mixed_second = [lax.optimization_barrier(jnp.sum(kernel * alpha_second[c], 1)) for c in range(3)]
    mixed_first = [lax.optimization_barrier(jnp.sum(kernel * alpha_first[c], 0)) for c in range(3)]
    turn_first = cross_list([first[3 + c] for c in range(3)], mixed_second)
    turn_second = cross_list([second[3 + c] for c in range(3)], mixed_first)
    str_first = [-inv_four_pi * (turn_first[c] - lax.optimization_barrier(jnp.sum(steep * proj_first * cross_second[c], 1))) for c in range(3)]
    str_second = [-inv_four_pi * (turn_second[c] - lax.optimization_barrier(jnp.sum(steep * proj_second * cross_first[c], 0))) for c in range(3)]
    return (jnp.stack(vel_first + str_first), jnp.stack(vel_second + str_second))

def reference(particles, pair_list, pair_count):
    blocks = jnp.moveaxis(particles.reshape(7, CLUSTERS, CLUSTER), 1, 0)
    total = lax.map(lambda block: interact(block, block)[0], blocks)
    slots = jnp.arange(RANKS * PAIR_CAP, dtype=jnp.int32)
    live = slots % PAIR_CAP < pair_count[slots // PAIR_CAP]

    def visit(carry, item):
        pair, alive = item
        first_id = pair[0]
        second_id = pair[1]
        upd_first, upd_second = interact(blocks[first_id], blocks[second_id])
        carry = carry.at[first_id].add(jnp.where(alive, upd_first, jnp.float32(0.0)))
        carry = carry.at[second_id].add(jnp.where(alive, upd_second, jnp.float32(0.0)))
        return (carry, None)
    total, unused = lax.scan(visit, total, (pair_list, live))
    result = jnp.moveaxis(total, 0, 1).reshape(6, PARTICLES)
    return (result[:3], result[3:])
```

```python
import jax
import jax.numpy as jnp
from jax import lax
from jax.experimental import pallas as pl
from jax.experimental.pallas import tpu as pltpu
from jax.sharding import PartitionSpec as P

CLUSTER = 512
REACH = 3
BATCH = 8
ROWS = 8
SUMS = 27
PADDED = 32
LANES = CLUSTER // 128
inv_four_pi = 0.07957747154594767
f32 = jnp.float32
bf16 = jnp.bfloat16


def passed_along(value, axis, steps):
    count = lax.axis_size(axis)
    first, last = (max(0, -steps), min(count, count - steps))
    return lax.ppermute(value, axis, [(source, source + steps) for source in range(first, last)])


def cross_list(left, right):
    return [
        left[1] * right[2] - left[2] * right[1],
        left[2] * right[0] - left[0] * right[2],
        left[0] * right[1] - left[1] * right[0],
    ]


def aligned(index, size):
    return pl.ds(pl.multiple_of(index * size, size), size)


def wide(ref, rows):
    return jnp.concatenate([ref[lane, rows, :] for lane in range(LANES)], axis=1)


def put(ref, rows, value):
    for lane in range(LANES):
        ref[lane, rows, :] = value[:, lane * 128 : lane * 128 + 128]


def prepare(window, block, here, table, centres, columns, moments, sources):
    x = [window[block, c] for c in range(3)]
    a = [window[block, 3 + c] for c in range(3)]
    core = window[block, 6]
    half = 0.5 * core * core
    middle = [jnp.mean(x[c], axis=1, keepdims=True) for c in range(3)]
    y = [x[c] - middle[c] for c in range(3)]
    first = block * here * ROWS
    for k, plane in enumerate([x[0], x[1], x[2], half, a[0], a[1], a[2], jnp.zeros_like(half)]):
        put(table, pl.ds(first + k, here, stride=ROWS), plane)
    for k in range(3):
        centres[pl.ds(first + k, here, stride=ROWS), :] = jnp.broadcast_to(middle[k], (here, 128))
    b = cross_list(y, a)
    size = y[0] * y[0] + y[1] * y[1] + y[2] * y[2] + half
    planes = a + [y[d] * a[c] for d in range(3) for c in range(3)]
    planes += [y[d] * b[c] for d in range(3) for c in range(3)]
    planes += [size * a[c] for c in range(3)] + [size * b[c] for c in range(3)]
    for k, plane in enumerate(planes):
        put(moments, pl.ds(k, here, stride=PADDED), plane)

    def split(index, _):
        cluster = block * here + index
        whole = wide(moments, aligned(index, PADDED))
        for part in range(3):
            piece = whole.astype(bf16)
            sources[cluster, part * PADDED : (part + 1) * PADDED, :] = piece
            whole = whole - piece.astype(f32)
        columns[cluster] = wide(table, aligned(cluster, ROWS)).T
        return 0

    lax.fori_loop(0, here, split, 0)


def steepness(target, source, table, columns, high, low, own):
    step = 128
    second = wide(table, aligned(source, ROWS))
    for row in range(0, CLUSTER, step):
        column = columns[target, row : row + step, :]
        radial = [column[:, c : c + 1] - second[c : c + 1, :] for c in range(3)]
        spread = column[:, 3:4] + second[3:4, :]
        rho = radial[0] * radial[0] + radial[1] * radial[1] + radial[2] * radial[2] + spread
        steep = jnp.exp2(-2.5 * jnp.log2(rho))
        if own:
            rows = lax.broadcasted_iota(jnp.int32, rho.shape, 0) + row
            steep = jnp.where(rows == lax.broadcasted_iota(jnp.int32, rho.shape, 1), 0.0, steep)
        piece = steep.astype(bf16)
        high[row : row + step, :] = piece
        low[row : row + step, :] = (steep - piece.astype(f32)).astype(bf16)


def matmul(left, right, side):
    return lax.dot_general(left, right, (((1,), (side,)), ((), ())), preferred_element_type=f32)


def folded(source, high, low, side):
    total = matmul(source, high, side) + matmul(source, low, side)
    return total[:PADDED] + total[PADDED : 2 * PADDED] + total[2 * PADDED :]


def combine(sums, targets, middles, answers):
    for lane in range(LANES):
        g = [sums[lane, pl.ds(k, BATCH, stride=PADDED), :] for k in range(SUMS)]
        t = [targets[lane, pl.ds(k, BATCH, stride=ROWS), :] for k in (0, 1, 2, 4, 5, 6, 3)]
        x = [t[c] - middles[pl.ds(c, BATCH, stride=ROWS), :] for c in range(3)]
        a = t[3:6]
        plain = g[0:3]
        ya = [g[3 + 3 * d : 6 + 3 * d] for d in range(3)]
        yb = [g[12 + 3 * d : 15 + 3 * d] for d in range(3)]
        b = [ya[1][2] - ya[2][1], ya[2][0] - ya[0][2], ya[0][1] - ya[1][0]]
        size = x[0] * x[0] + x[1] * x[1] + x[2] * x[2] + t[6]
        twice = [2.0 * x[c] for c in range(3)]

        def along(vector, matrix, c):
            return vector[0] * matrix[0][c] + vector[1] * matrix[1][c] + vector[2] * matrix[2][c]

        ka = [size * plain[c] + (g[21 + c] - along(twice, ya, c)) for c in range(3)]
        kb = [size * b[c] + (g[24 + c] - along(twice, yb, c)) for c in range(3)]
        project = a[0] * x[0] + a[1] * x[1] + a[2] * x[2]
        q = [project * plain[c] - along(a, ya, c) for c in range(3)]
        r = [project * b[c] - along(a, yb, c) for c in range(3)]
        turn = cross_list(a, ka)
        moved = cross_list(x, ka)
        tilt = cross_list(x, q)
        for c in range(3):
            answers[lane, pl.ds(c, BATCH, stride=ROWS), :] = -inv_four_pi * (moved[c] - kb[c])
            answers[lane, pl.ds(3 + c, BATCH, stride=ROWS), :] = -inv_four_pi * (
                turn[c] - 3.0 * (tilt[c] - r[c])
            )


def kernel(
    pairs, count, window, out,
    table, centres, columns, moments, sources, total,
    high0, low0, high1, low1, sums_first, sums_second, targets, middles, answers,
):
    blocks = window.shape[0]
    here = window.shape[2]
    moments[...] = jnp.zeros_like(moments)
    total[...] = jnp.zeros_like(total)
    answers[...] = jnp.zeros_like(answers)
    for block in range(blocks):
        prepare(window, block, here, table, centres, columns, moments, sources)
    high, low = (high0, high1), (low0, low1)

    def spread_out(target_of, source_of, sums, live_of):
        for slot in range(BATCH):
            targets[:, slot * ROWS : (slot + 1) * ROWS, :] = table[:, aligned(target_of(slot), ROWS), :]
            middles[slot * ROWS : (slot + 1) * ROWS, :] = centres[aligned(source_of(slot), ROWS), :]
        combine(sums, targets, middles, answers)
        for slot in range(BATCH):

            @pl.when(live_of(slot))
            def _():
                where = aligned(target_of(slot), ROWS)
                total[:, where, :] += answers[:, slot * ROWS : (slot + 1) * ROWS, :]

    def own_batch(batch, _):
        def own_pair(turn, _):
            for h in range(2):
                slot = turn * 2 + h
                cluster = REACH * here + batch * BATCH + slot
                steepness(cluster, cluster, table, columns, high[h], low[h], True)
                put(
                    sums_first,
                    aligned(slot, PADDED),
                    folded(sources[cluster], high[h][...], low[h][...], 0),
                )
            return 0

        lax.fori_loop(0, BATCH // 2, own_pair, 0)
        own = lambda slot: REACH * here + batch * BATCH + slot
        spread_out(own, own, sums_first, lambda slot: slot >= 0)
        return 0

    lax.fori_loop(0, here // BATCH, own_batch, 0)

    live = count[0]
    device = lax.axis_index(("gx", "gy"))
    anchor = (device - REACH) * here

    def chosen(unit, side):
        held = jnp.clip(unit, 0, live - 1)
        return jnp.clip(pairs[held, side] - anchor, 0, blocks * here - 1)

    def pair_batch(batch, _):
        def pair_turn(turn, _):
            base = batch * BATCH + turn * 2
            for h in range(2):
                steepness(
                    chosen(base + h, 0), chosen(base + h, 1), table, columns, high[h], low[h], False
                )
                before = base + h - 1
                slot = turn * 2 + h
                hi, lo = high[1 - h][...], low[1 - h][...]
                put(sums_second, aligned(slot, PADDED), folded(sources[chosen(before, 0)], hi, lo, 0))
                put(sums_first, aligned(slot, PADDED), folded(sources[chosen(before, 1)], hi, lo, 1))
            return 0

        lax.fori_loop(0, BATCH // 2, pair_turn, 0)
        unit = lambda slot: batch * BATCH + slot - 1
        alive = lambda slot: jnp.logical_and(unit(slot) >= 0, unit(slot) < live)
        one = lambda slot: chosen(unit(slot), 0)
        two = lambda slot: chosen(unit(slot), 1)
        spread_out(one, two, sums_first, alive)
        spread_out(two, one, sums_second, alive)
        return 0

    lax.fori_loop(0, (live + BATCH) // BATCH, pair_batch, 0)

    for block in range(blocks):
        for k in range(6):
            out[block, k] = wide(total, pl.ds(block * here * ROWS + k, here, stride=ROWS))


def near_field(window, pair_list, pair_count):
    blocks, _, here, _ = window.shape
    clusters = blocks * here
    square = pltpu.VMEM((CLUSTER, CLUSTER), bf16)
    return pl.pallas_call(
        kernel,
        out_shape=jax.ShapeDtypeStruct((blocks, 6, here, CLUSTER), f32),
        in_specs=[
            pl.BlockSpec(memory_space=pltpu.SMEM),
            pl.BlockSpec(memory_space=pltpu.SMEM),
            pl.BlockSpec(memory_space=pltpu.VMEM),
        ],
        out_specs=pl.BlockSpec(memory_space=pltpu.VMEM),
        scratch_shapes=[
            pltpu.VMEM((LANES, clusters * ROWS, 128), f32),
            pltpu.VMEM((clusters * ROWS, 128), f32),
            pltpu.VMEM((clusters, CLUSTER, ROWS), f32),
            pltpu.VMEM((LANES, here * PADDED, 128), f32),
            pltpu.VMEM((clusters, 3 * PADDED, CLUSTER), bf16),
            pltpu.VMEM((LANES, clusters * ROWS, 128), f32),
            square, square, square, square,
            pltpu.VMEM((LANES, BATCH * PADDED, 128), f32),
            pltpu.VMEM((LANES, BATCH * PADDED, 128), f32),
            pltpu.VMEM((LANES, BATCH * ROWS, 128), f32),
            pltpu.VMEM((BATCH * ROWS, 128), f32),
            pltpu.VMEM((LANES, BATCH * ROWS, 128), f32),
        ],
        compiler_params=pltpu.CompilerParams(vmem_limit_bytes=58 * 2**20),
        name="near_field",
    )(pair_list, pair_count, window)


def shards(particles, pair_list, pair_count):
    width = particles.shape[1]
    here = width // CLUSTER
    owned = particles.reshape(7, here, CLUSTER)
    axis = ("gx", "gy")
    around = {0: owned}
    for offset in list(range(-REACH, 0)) + list(range(1, REACH + 1)):
        around[offset] = passed_along(owned, axis, -offset)
    window = jnp.stack([around[offset] for offset in range(-REACH, REACH + 1)])
    pieces = near_field(window, pair_list, pair_count)
    result = pieces[REACH]
    for offset in list(range(-REACH, 0)) + list(range(1, REACH + 1)):
        result = result + passed_along(pieces[offset + REACH], axis, offset)
    final = result.reshape(6, width)
    return (final[:3], final[3:])


def solution(mesh):
    placed = (P(None, ("gx", "gy")), P(("gx", "gy"), None), P(("gx", "gy")))
    return jax.shard_map(
        shards,
        mesh=mesh,
        in_specs=placed,
        out_specs=(P(None, ("gx", "gy")), P(None, ("gx", "gy"))),
        check_vma=False,
    )
```

```python
import functools

import jax
import jax.numpy as jnp
from jax import lax
from jax.experimental import pallas as pl
from jax.experimental.pallas import tpu as pltpu
from jax.sharding import PartitionSpec as P

CLUSTER = 512
REACH = 3
BATCH = 8
ROWS = 8
SUMS = 27
STRIP = 128
PADDED = 32
LANES = CLUSTER // 128
inv_four_pi = 0.07957747154594767
f32 = jnp.float32
bf16 = jnp.bfloat16


def passed_along(value, axis, steps):
    count = lax.axis_size(axis)
    first, last = (max(0, -steps), min(count, count - steps))
    return lax.ppermute(value, axis, [(source, source + steps) for source in range(first, last)])


def cross_list(left, right):
    return [
        left[1] * right[2] - left[2] * right[1],
        left[2] * right[0] - left[0] * right[2],
        left[0] * right[1] - left[1] * right[0],
    ]


def aligned(index, size):
    return pl.ds(pl.multiple_of(index * size, size), size)


def wide(ref, rows):
    return jnp.concatenate([ref[lane, rows, :] for lane in range(LANES)], axis=1)


def put(ref, rows, value, *lead):
    for lane in range(LANES):
        ref[(*lead, lane, rows, slice(None))] = value[:, lane * 128 : lane * 128 + 128]


def prepare(window, block, here, table, centres, moments, sources):
    x = [window[block, c] for c in range(3)]
    a = [window[block, 3 + c] for c in range(3)]
    core = window[block, 6]
    half = 0.5 * core * core
    middle = [jnp.mean(x[c], axis=1, keepdims=True) for c in range(3)]
    y = [x[c] - middle[c] for c in range(3)]
    first = block * here * ROWS
    for k, plane in enumerate([x[0], x[1], x[2], half, a[0], a[1], a[2], jnp.zeros_like(half)]):
        put(table, pl.ds(first + k, here, stride=ROWS), plane)
    for k in range(3):
        centres[pl.ds(first + k, here, stride=ROWS), :] = jnp.broadcast_to(middle[k], (here, 128))
    b = cross_list(y, a)
    size = y[0] * y[0] + y[1] * y[1] + y[2] * y[2] + half
    planes = a + [y[d] * a[c] for d in range(3) for c in range(3)]
    planes += [y[d] * b[c] for d in range(3) for c in range(3)]
    planes += [size * a[c] for c in range(3)] + [size * b[c] for c in range(3)]
    for k, plane in enumerate(planes):
        put(moments, pl.ds(k, here, stride=PADDED), plane)

    def split(turn, _):
        for index in [turn * 4 + k for k in range(4)]:
            whole = wide(moments, aligned(index, PADDED))
            for part in range(3):
                piece = whole.astype(bf16)
                sources[block * here + index, part * PADDED : (part + 1) * PADDED, :] = piece
                whole = whole - piece.astype(f32)
        return 0

    lax.fori_loop(0, here // 4, split, 0)


def parted(rows):
    high = rows.astype(bf16).astype(f32)
    rest = rows - high
    middle = rest.astype(bf16).astype(f32)
    return high, middle, rest - middle


def features(rows, middle, left):
    place = lax.broadcasted_iota(jnp.int32, rows.shape, 0)
    moved = rows - jnp.concatenate([middle] * LANES, axis=1)
    size = jnp.where(place < 3, moved * moved, jnp.where(place == 3, moved, 0.0))
    size = jnp.sum(size, axis=0, keepdims=True)
    if left:
        whole = jnp.where(place < 3, moved, jnp.where(place == 3, size, jnp.where(place == 4, 1.0, 0.0)))
        h, m, l = parted(whole)
        return jnp.concatenate([h, h, m, m, h, l], axis=0)
    whole = jnp.where(place < 3, -2.0 * moved, jnp.where(place == 3, 1.0, jnp.where(place == 4, size, 0.0)))
    h, m, l = parted(whole)
    return jnp.concatenate([h, m, h, m, l, h], axis=0)


def steepness(target, source, table, centres, high, low, high_across=None, low_across=None):
    step = STRIP
    second = wide(table, aligned(source, ROWS))
    middle = centres[aligned(target, ROWS), :]
    left = features(wide(table, aligned(target, ROWS)), middle, True).T.astype(bf16)
    right = features(second, middle, False).astype(bf16)
    for row in range(0, CLUSTER, step):
        rho = jnp.maximum(matmul(left[row : row + step], right), second[3:4, :])
        inverse = lax.rsqrt(rho)
        square = inverse * inverse
        steep = square * square * inverse
        if high_across is None:
            rows = lax.broadcasted_iota(jnp.int32, rho.shape, 0) + row
            steep = jnp.where(rows == lax.broadcasted_iota(jnp.int32, rho.shape, 1), 0.0, steep)
        piece = steep.astype(bf16)
        rest = (steep - piece.astype(f32)).astype(bf16)
        high[row : row + step, :] = piece
        low[row : row + step, :] = rest
        if high_across is not None:
            high_across[:, row : row + step] = piece.T
            low_across[:, row : row + step] = rest.T


def matmul(left, right):
    return lax.dot_general(left, right, (((1,), (0,)), ((), ())), preferred_element_type=f32)


def folded(source, high, low):
    total = matmul(source, high) + matmul(source, low)
    return total[:PADDED] + total[PADDED : 2 * PADDED] + total[2 * PADDED :]


def combine(sums, parity, lane, targets, middles, answers):
    g = [sums[parity, lane, pl.ds(k, BATCH, stride=PADDED), :] for k in range(SUMS)]
    t = [targets[pl.ds(k, BATCH, stride=ROWS), :] for k in (0, 1, 2, 4, 5, 6, 3)]
    x = [t[c] - middles[pl.ds(c, BATCH, stride=ROWS), :] for c in range(3)]
    a = t[3:6]
    plain = g[0:3]
    ya = [g[3 + 3 * d : 6 + 3 * d] for d in range(3)]
    yb = [g[12 + 3 * d : 15 + 3 * d] for d in range(3)]
    b = [ya[1][2] - ya[2][1], ya[2][0] - ya[0][2], ya[0][1] - ya[1][0]]
    size = x[0] * x[0] + x[1] * x[1] + x[2] * x[2] + t[6]
    twice = [2.0 * x[c] for c in range(3)]

    def along(vector, matrix, c):
        return vector[0] * matrix[0][c] + vector[1] * matrix[1][c] + vector[2] * matrix[2][c]

    ka = [size * plain[c] + (g[21 + c] - along(twice, ya, c)) for c in range(3)]
    kb = [size * b[c] + (g[24 + c] - along(twice, yb, c)) for c in range(3)]
    project = a[0] * x[0] + a[1] * x[1] + a[2] * x[2]
    q = [project * plain[c] - along(a, ya, c) for c in range(3)]
    r = [project * b[c] - along(a, yb, c) for c in range(3)]
    turn = cross_list(a, ka)
    moved = cross_list(x, ka)
    tilt = cross_list(x, q)
    for c in range(3):
        answers[pl.ds(c, BATCH, stride=ROWS), :] = -inv_four_pi * (moved[c] - kb[c])
        answers[pl.ds(3 + c, BATCH, stride=ROWS), :] = -inv_four_pi * (
            turn[c] - 3.0 * (tilt[c] - r[c])
        )


def settle(target_of, source_of, live_of, sums, parity, lane, table, centres, total, room):
    targets, middles, answers = room
    for slot in range(BATCH):
        targets[slot * ROWS : (slot + 1) * ROWS, :] = table[lane, aligned(target_of(slot), ROWS), :]
        middles[slot * ROWS : (slot + 1) * ROWS, :] = centres[aligned(source_of(slot), ROWS), :]
    combine(sums, parity, lane, targets, middles, answers)
    for slot in range(BATCH):
        update = answers[slot * ROWS : (slot + 1) * ROWS, :]
        if live_of is not None:
            update = jnp.where(live_of(slot), update, 0.0)
        total[lane, aligned(target_of(slot), ROWS), :] += update


def begin(window, table, centres, moments, sources, total):
    blocks, _, here, _ = window.shape
    moments[...] = jnp.zeros_like(moments)
    centres[...] = jnp.zeros_like(centres)
    total[...] = jnp.zeros_like(total)
    for block in range(blocks):
        prepare(window, block, here, table, centres, moments, sources)


def finish(total, out):
    blocks, _, here, _ = out.shape
    for block in range(blocks):
        for k in range(6):
            out[block, k] = wide(total, pl.ds(block * here * ROWS + k, here, stride=ROWS))


def own_kernel(
    pairs, count, start, window, out, order, bounds,
    table, centres, moments, sources, total, high0, low0, high1, low1, sums, targets, middles, answers,
):
    here = window.shape[2]
    live = count[0]
    anchor = start[0]
    last = (2 * REACH + 1) * here - 1

    def place(slot, front):
        first = jnp.clip(pairs[slot, 0] - anchor, 0, last)
        second = jnp.clip(pairs[slot, 1] - anchor, 0, last)
        inner = jnp.logical_and(first >= REACH * here, second < (REACH + 1) * here)
        inner = jnp.logical_and(inner, jnp.logical_and(second >= REACH * here, first < (REACH + 1) * here))
        where = jnp.where(inner, live - 1 - (slot - front), front)
        order[where, 0] = first
        order[where, 1] = second
        return front + jnp.where(inner, 0, 1)

    bounds[0] = lax.fori_loop(0, live, place, 0)
    bounds[1] = live
    begin(window, table, centres, moments, sources, total)
    answers[...] = jnp.zeros_like(answers)
    high, low = (high0, high1), (low0, low1)
    steepness(0, 0, table, centres, high0, low0)

    def own_turn(turn, _):
        for h in range(2):
            cluster = turn * 2 + h
            following = jnp.minimum(cluster + 1, here - 1)
            steepness(following, following, table, centres, high[1 - h], low[1 - h])
            answer = folded(sources[cluster], high[h][...], low[h][...])
            put(sums, aligned(lax.rem(cluster, BATCH), PADDED), answer, lax.div(cluster, BATCH))
        return 0

    lax.fori_loop(0, here // 2, own_turn, 0)

    def own_settle(batch, _):
        own = lambda slot: batch * BATCH + slot
        for lane in range(LANES):
            settle(own, own, None, sums, batch, lane, table, centres, total, (targets, middles, answers))
        return 0

    lax.fori_loop(0, here // BATCH, own_settle, 0)
    finish(total, out)


def pair_kernel(
    shift, inner, order, bounds, window, out,
    table, centres, moments, sources, total, high0, low0, high1, low1,
    high_across0, low_across0, high_across1, low_across1, sums_first, sums_second, *rooms,
):
    blocks, _, here, _ = window.shape
    begin(window, table, centres, moments, sources, total)
    room_first, room_second = rooms[:3], rooms[3:]
    for room in (room_first, room_second):
        room[2][...] = jnp.zeros_like(room[2])
    for square in (high1, low1, high_across1, low_across1):
        square[...] = jnp.zeros_like(square)
    squares = (
        (high0, low0, high_across0, low_across0),
        (high1, low1, high_across1, low_across1),
    )
    first_unit = bounds[0] if inner else 0
    end_unit = bounds[1] if inner else bounds[0]

    def chosen(unit, side):
        held = jnp.maximum(jnp.clip(unit, first_unit, end_unit - 1), 0)
        return jnp.clip(order[held, side] - shift, 0, blocks * here - 1)

    def settle_part(turn):
        batch = lax.div(turn, BATCH // 2) - 1
        lane = lax.rem(turn, BATCH // 2)
        parity = lax.rem(batch + 2, 2)
        unit = lambda slot: first_unit + batch * BATCH + slot - 1
        alive = lambda slot: jnp.logical_and(unit(slot) >= first_unit, unit(slot) < end_unit)
        one = lambda slot: chosen(unit(slot), 0)
        two = lambda slot: chosen(unit(slot), 1)
        settle(one, two, alive, sums_first, parity, lane, table, centres, total, room_first)
        settle(two, one, alive, sums_second, parity, lane, table, centres, total, room_second)

    def pair_turn(turn, _):
        base = first_unit + turn * 2
        parity = lax.rem(lax.div(turn, BATCH // 2), 2)
        for h in range(2):
            steepness(chosen(base + h, 0), chosen(base + h, 1), table, centres, *squares[h])
            before = base + h - 1
            rows = aligned(lax.rem(turn, BATCH // 2) * 2 + h, PADDED)
            hi, lo, hi_across, lo_across = [ref[...] for ref in squares[1 - h]]
            put(sums_second, rows, folded(sources[chosen(before, 0)], hi, lo), parity)
            put(sums_first, rows, folded(sources[chosen(before, 1)], hi_across, lo_across), parity)
        settle_part(turn)
        return 0

    def settle_turn(turn, _):
        settle_part(turn)
        return 0

    turns = lax.div(end_unit - first_unit + 2, 2)
    lax.fori_loop(0, turns, pair_turn, 0)
    quarter = BATCH // 2
    lax.fori_loop(turns, lax.div(turns + quarter - 1, quarter) * quarter + quarter, settle_turn, 0)
    finish(total, out)


def tables(clusters, here):
    return [
        pltpu.VMEM((LANES, clusters * ROWS, 128), f32),
        pltpu.VMEM((clusters * ROWS, 128), f32),
        pltpu.VMEM((LANES, here * PADDED, 128), f32),
        pltpu.VMEM((clusters, 3 * PADDED, CLUSTER), bf16),
        pltpu.VMEM((LANES, clusters * ROWS, 128), f32),
    ]


in_scalars = pl.BlockSpec(memory_space=pltpu.SMEM)
in_vectors = pl.BlockSpec(memory_space=pltpu.VMEM)
square = pltpu.VMEM((CLUSTER, CLUSTER), bf16)
room = [pltpu.VMEM((BATCH * ROWS, 128), f32)] * 3


def own_terms(owned, pair_list, pair_count, anchor):
    here = owned.shape[2]
    return pl.pallas_call(
        own_kernel,
        out_shape=[
            jax.ShapeDtypeStruct((1, 6, here, CLUSTER), f32),
            jax.ShapeDtypeStruct(pair_list.shape, jnp.int32),
            jax.ShapeDtypeStruct((2,), jnp.int32),
        ],
        in_specs=[in_scalars, in_scalars, in_scalars, in_vectors],
        out_specs=[in_vectors, in_scalars, in_scalars],
        scratch_shapes=tables(here, here)
        + [square] * 4
        + [pltpu.VMEM((here // BATCH, LANES, BATCH * PADDED, 128), f32)]
        + room,
        compiler_params=pltpu.CompilerParams(vmem_limit_bytes=32 * 2**20),
        cost_estimate=pl.CostEstimate(flops=12 * 10**9, bytes_accessed=10**6, transcendentals=0),
        name="own_terms",
    )(pair_list, pair_count, anchor, owned)


def pair_terms(window, order, bounds, inner):
    blocks, _, here, _ = window.shape
    clusters = blocks * here
    sums = pltpu.VMEM((2, LANES, BATCH * PADDED, 128), f32)
    return pl.pallas_call(
        functools.partial(pair_kernel, REACH * here if inner else 0, inner),
        out_shape=jax.ShapeDtypeStruct((blocks, 6, here, CLUSTER), f32),
        in_specs=[in_scalars, in_scalars, in_vectors],
        out_specs=in_vectors,
        scratch_shapes=tables(clusters, here) + [square] * 8 + [sums] * 2 + room * 2,
        compiler_params=pltpu.CompilerParams(vmem_limit_bytes=50 * 2**20),
        cost_estimate=pl.CostEstimate(
            flops=(16 if inner else 150) * 10**9, bytes_accessed=10**6, transcendentals=0
        ),
        name="inner_pairs" if inner else "outer_pairs",
    )(order, bounds, window)


def shards(particles, pair_list, pair_count):
    width = particles.shape[1]
    here = width // CLUSTER
    owned = particles.reshape(7, here, CLUSTER)
    axis = ("gx", "gy")
    others = list(range(-REACH, 0)) + list(range(1, REACH + 1))
    around = {0: owned}
    for offset in others:
        around[offset] = passed_along(owned, axis, -offset)
    anchor = ((lax.axis_index(axis) - REACH) * here).astype(jnp.int32).reshape(1)
    alone, order, bounds = own_terms(owned[None], pair_list, pair_count, anchor)
    window = jnp.stack([around[offset] for offset in range(-REACH, REACH + 1)])
    pieces = pair_terms(window, order, bounds, False)
    inner = pair_terms(owned[None], order, bounds, True)
    result = alone[0] + inner[0] + pieces[REACH]
    for offset in others:
        result = result + passed_along(pieces[offset + REACH], axis, offset)
    final = result.reshape(6, width)
    return (final[:3], final[3:])


def solution(mesh):
    placed = (P(None, ("gx", "gy")), P(("gx", "gy"), None), P(("gx", "gy")))
    return jax.shard_map(
        shards,
        mesh=mesh,
        in_specs=placed,
        out_specs=(P(None, ("gx", "gy")), P(None, ("gx", "gy"))),
        check_vma=False,
    )
```

```python
import functools

import jax
import jax.numpy as jnp
from jax import lax
from jax.experimental import pallas as pl
from jax.experimental.pallas import tpu as pltpu
from jax.sharding import PartitionSpec as P

CLUSTER = 512
REACH = 3
BATCH = 8
ROWS = 8
SUMS = 27
STRIP = 256
LATE = 24
PADDED = 32
LANES = CLUSTER // 128
inv_four_pi = 0.07957747154594767
f32 = jnp.float32
bf16 = jnp.bfloat16


def passed_along(value, axis, steps):
    count = lax.axis_size(axis)
    first, last = (max(0, -steps), min(count, count - steps))
    return lax.ppermute(value, axis, [(source, source + steps) for source in range(first, last)])


def cross_list(left, right):
    return [
        left[1] * right[2] - left[2] * right[1],
        left[2] * right[0] - left[0] * right[2],
        left[0] * right[1] - left[1] * right[0],
    ]


def aligned(index, size):
    return pl.ds(pl.multiple_of(index * size, size), size)


def wide(ref, rows):
    return jnp.concatenate([ref[lane, rows, :] for lane in range(LANES)], axis=1)


def put(ref, rows, value, *lead):
    for lane in range(LANES):
        ref[(*lead, lane, rows, slice(None))] = value[:, lane * 128 : lane * 128 + 128]


def prepare(window, block, here, table, centres, moments, sources):
    x = [window[block, c] for c in range(3)]
    a = [window[block, 3 + c] for c in range(3)]
    core = window[block, 6]
    half = 0.5 * core * core
    middle = [jnp.mean(x[c], axis=1, keepdims=True) for c in range(3)]
    y = [x[c] - middle[c] for c in range(3)]
    first = block * here * ROWS
    for k, plane in enumerate([x[0], x[1], x[2], half, a[0], a[1], a[2], jnp.zeros_like(half)]):
        put(table, pl.ds(first + k, here, stride=ROWS), plane)
    for k in range(3):
        centres[pl.ds(first + k, here, stride=ROWS), :] = jnp.broadcast_to(middle[k], (here, 128))
    b = cross_list(y, a)
    size = y[0] * y[0] + y[1] * y[1] + y[2] * y[2] + half
    planes = a + [y[d] * a[c] for d in range(3) for c in range(3)]
    planes += [y[d] * b[c] for d in range(3) for c in range(3)]
    planes += [size * a[c] for c in range(3)] + [size * b[c] for c in range(3)]
    for k, plane in enumerate(planes):
        put(moments, pl.ds(k, here, stride=PADDED), plane)

    def split(turn, _):
        for index in [turn * 4 + k for k in range(4)]:
            whole = wide(moments, aligned(index, PADDED))
            for part in range(3):
                piece = whole.astype(bf16)
                sources[block * here + index, part * PADDED : (part + 1) * PADDED, :] = piece
                whole = whole - piece.astype(f32)
        return 0

    lax.fori_loop(0, here // 4, split, 0)


def parted(rows):
    high = rows.astype(bf16).astype(f32)
    rest = rows - high
    middle = rest.astype(bf16).astype(f32)
    return high, middle, rest - middle


def features(rows, middle, left):
    place = lax.broadcasted_iota(jnp.int32, rows.shape, 0)
    moved = rows - jnp.concatenate([middle] * LANES, axis=1)
    size = jnp.where(place < 3, moved * moved, jnp.where(place == 3, moved, 0.0))
    size = jnp.sum(size, axis=0, keepdims=True)
    if left:
        whole = jnp.where(place < 3, moved, jnp.where(place == 3, size, jnp.where(place == 4, 1.0, 0.0)))
        h, m, l = parted(whole)
        return jnp.concatenate([h, h, m, m, h, l], axis=0)
    whole = jnp.where(place < 3, -2.0 * moved, jnp.where(place == 3, 1.0, jnp.where(place == 4, size, 0.0)))
    h, m, l = parted(whole)
    return jnp.concatenate([h, m, h, m, l, h], axis=0)


def steepness(target, source, table, centres, high, low, high_across=None, low_across=None):
    step = STRIP
    second = wide(table, aligned(source, ROWS))
    middle = centres[aligned(target, ROWS), :]
    left = features(wide(table, aligned(target, ROWS)), middle, True).astype(bf16).T
    right = features(second, middle, False).astype(bf16)
    for row in range(0, CLUSTER, step):
        rho = jnp.maximum(matmul(left[row : row + step], right), second[3:4, :])
        inverse = lax.rsqrt(rho)
        square = inverse * inverse
        steep = square * square * inverse
        if high_across is None:
            rows = lax.broadcasted_iota(jnp.int32, rho.shape, 0) + row
            steep = jnp.where(rows == lax.broadcasted_iota(jnp.int32, rho.shape, 1), 0.0, steep)
        piece = steep.astype(bf16)
        rest = (steep - piece.astype(f32)).astype(bf16)
        high[row : row + step, :] = piece
        low[row : row + step, :] = rest
        if high_across is not None:
            high_across[:, row : row + step] = piece.T
            low_across[:, row : row + step] = rest.T


def matmul(left, right):
    return lax.dot_general(left, right, (((1,), (0,)), ((), ())), preferred_element_type=f32)


def folded(source, high, low):
    total = matmul(source, high) + matmul(source, low)
    return total[:PADDED] + total[PADDED : 2 * PADDED] + total[2 * PADDED :]


def combine(sums, parity, lane, targets, middles, answers):
    g = [sums[parity, lane, pl.ds(k, BATCH, stride=PADDED), :] for k in range(SUMS)]
    t = [targets[pl.ds(k, BATCH, stride=ROWS), :] for k in (0, 1, 2, 4, 5, 6, 3)]
    x = [t[c] - middles[pl.ds(c, BATCH, stride=ROWS), :] for c in range(3)]
    a = t[3:6]
    plain = g[0:3]
    ya = [g[3 + 3 * d : 6 + 3 * d] for d in range(3)]
    yb = [g[12 + 3 * d : 15 + 3 * d] for d in range(3)]
    b = [ya[1][2] - ya[2][1], ya[2][0] - ya[0][2], ya[0][1] - ya[1][0]]
    size = x[0] * x[0] + x[1] * x[1] + x[2] * x[2] + t[6]
    twice = [2.0 * x[c] for c in range(3)]

    def along(vector, matrix, c):
        return vector[0] * matrix[0][c] + vector[1] * matrix[1][c] + vector[2] * matrix[2][c]

    ka = [size * plain[c] + (g[21 + c] - along(twice, ya, c)) for c in range(3)]
    kb = [size * b[c] + (g[24 + c] - along(twice, yb, c)) for c in range(3)]
    project = a[0] * x[0] + a[1] * x[1] + a[2] * x[2]
    q = [project * plain[c] - along(a, ya, c) for c in range(3)]
    r = [project * b[c] - along(a, yb, c) for c in range(3)]
    turn = cross_list(a, ka)
    moved = cross_list(x, ka)
    tilt = cross_list(x, q)
    for c in range(3):
        answers[pl.ds(c, BATCH, stride=ROWS), :] = -inv_four_pi * (moved[c] - kb[c])
        answers[pl.ds(3 + c, BATCH, stride=ROWS), :] = -inv_four_pi * (
            turn[c] - 3.0 * (tilt[c] - r[c])
        )


def settle(target_of, source_of, live_of, sums, parity, lane, table, centres, total, room):
    targets, middles, answers = room
    for slot in range(BATCH):
        targets[slot * ROWS : (slot + 1) * ROWS, :] = table[lane, aligned(target_of(slot), ROWS), :]
        middles[slot * ROWS : (slot + 1) * ROWS, :] = centres[aligned(source_of(slot), ROWS), :]
    combine(sums, parity, lane, targets, middles, answers)
    for slot in range(BATCH):
        update = answers[slot * ROWS : (slot + 1) * ROWS, :]
        if live_of is not None:
            update = jnp.where(live_of(slot), update, 0.0)
        total[lane, aligned(target_of(slot), ROWS), :] += update


def begin(window, table, centres, moments, sources, total):
    blocks, _, here, _ = window.shape
    moments[...] = jnp.zeros_like(moments)
    centres[...] = jnp.zeros_like(centres)
    total[...] = jnp.zeros_like(total)
    for block in range(blocks):
        prepare(window, block, here, table, centres, moments, sources)


def finish(total, out):
    blocks, _, here, _ = out.shape
    for block in range(blocks):
        for k in range(6):
            out[block, k] = wide(total, pl.ds(block * here * ROWS + k, here, stride=ROWS))


def own_kernel(
    pairs, count, start, window, out, order, bounds,
    table, centres, moments, sources, total, high0, low0, high1, low1, sums, targets, middles, answers,
):
    here = window.shape[2]
    live = count[0]
    anchor = start[0]
    last = (2 * REACH + 1) * here - 1

    def place(slot, front):
        first = jnp.clip(pairs[slot, 0] - anchor, 0, last)
        second = jnp.clip(pairs[slot, 1] - anchor, 0, last)
        inner = jnp.logical_and(first >= REACH * here, second < (REACH + 1) * here)
        inner = jnp.logical_and(inner, jnp.logical_and(second >= REACH * here, first < (REACH + 1) * here))
        inner = jnp.logical_and(inner, slot - front < LATE)
        where = jnp.where(inner, live - 1 - (slot - front), front)
        order[where, 0] = first
        order[where, 1] = second
        return front + jnp.where(inner, 0, 1)

    bounds[0] = lax.fori_loop(0, live, place, 0)
    bounds[1] = live
    begin(window, table, centres, moments, sources, total)
    answers[...] = jnp.zeros_like(answers)
    high, low = (high0, high1), (low0, low1)
    steepness(0, 0, table, centres, high0, low0)

    def own_turn(turn, _):
        for h in range(2):
            cluster = turn * 2 + h
            following = jnp.minimum(cluster + 1, here - 1)
            steepness(following, following, table, centres, high[1 - h], low[1 - h])
            answer = folded(sources[cluster], high[h][...], low[h][...])
            put(sums, aligned(lax.rem(cluster, BATCH), PADDED), answer, lax.div(cluster, BATCH))
        return 0

    lax.fori_loop(0, here // 2, own_turn, 0)

    def own_settle(batch, _):
        own = lambda slot: batch * BATCH + slot
        for lane in range(LANES):
            settle(own, own, None, sums, batch, lane, table, centres, total, (targets, middles, answers))
        return 0

    lax.fori_loop(0, here // BATCH, own_settle, 0)
    finish(total, out)


def pair_kernel(
    shift, inner, order, bounds, window, out,
    table, centres, moments, sources, total, high0, low0, high1, low1,
    high_across0, low_across0, high_across1, low_across1, sums_first, sums_second, *rooms,
):
    blocks, _, here, _ = window.shape
    begin(window, table, centres, moments, sources, total)
    room_first, room_second = rooms[:3], rooms[3:]
    for room in (room_first, room_second):
        room[2][...] = jnp.zeros_like(room[2])
    for square in (high1, low1, high_across1, low_across1):
        square[...] = jnp.zeros_like(square)
    squares = (
        (high0, low0, high_across0, low_across0),
        (high1, low1, high_across1, low_across1),
    )
    first_unit = bounds[0] if inner else 0
    end_unit = bounds[1] if inner else bounds[0]

    def chosen(unit, side):
        held = jnp.maximum(jnp.clip(unit, first_unit, end_unit - 1), 0)
        return jnp.clip(order[held, side] - shift, 0, blocks * here - 1)

    def settle_part(turn):
        batch = lax.div(turn, BATCH // 2) - 1
        lane = lax.rem(turn, BATCH // 2)
        parity = lax.rem(batch + 2, 2)
        unit = lambda slot: first_unit + batch * BATCH + slot - 1
        alive = lambda slot: jnp.logical_and(unit(slot) >= first_unit, unit(slot) < end_unit)
        one = lambda slot: chosen(unit(slot), 0)
        two = lambda slot: chosen(unit(slot), 1)
        settle(one, two, alive, sums_first, parity, lane, table, centres, total, room_first)
        settle(two, one, alive, sums_second, parity, lane, table, centres, total, room_second)

    def pair_turn(turn, _):
        base = first_unit + turn * 2
        parity = lax.rem(lax.div(turn, BATCH // 2), 2)
        for h in range(2):
            steepness(chosen(base + h, 0), chosen(base + h, 1), table, centres, *squares[h])
            before = base + h - 1
            rows = aligned(lax.rem(turn, BATCH // 2) * 2 + h, PADDED)
            hi, lo, hi_across, lo_across = [ref[...] for ref in squares[1 - h]]
            put(sums_second, rows, folded(sources[chosen(before, 0)], hi, lo), parity)
            put(sums_first, rows, folded(sources[chosen(before, 1)], hi_across, lo_across), parity)
        settle_part(turn)
        return 0

    def settle_turn(turn, _):
        settle_part(turn)
        return 0

    turns = lax.div(end_unit - first_unit + 2, 2)
    lax.fori_loop(0, turns, pair_turn, 0)
    quarter = BATCH // 2
    lax.fori_loop(turns, lax.div(turns + quarter - 1, quarter) * quarter + quarter, settle_turn, 0)
    finish(total, out)


def tables(clusters, here):
    return [
        pltpu.VMEM((LANES, clusters * ROWS, 128), f32),
        pltpu.VMEM((clusters * ROWS, 128), f32),
        pltpu.VMEM((LANES, here * PADDED, 128), f32),
        pltpu.VMEM((clusters, 3 * PADDED, CLUSTER), bf16),
        pltpu.VMEM((LANES, clusters * ROWS, 128), f32),
    ]


in_scalars = pl.BlockSpec(memory_space=pltpu.SMEM)
in_vectors = pl.BlockSpec(memory_space=pltpu.VMEM)
square = pltpu.VMEM((CLUSTER, CLUSTER), bf16)
room = [pltpu.VMEM((BATCH * ROWS, 128), f32)] * 3


def own_terms(owned, pair_list, pair_count, anchor):
    here = owned.shape[2]
    return pl.pallas_call(
        own_kernel,
        out_shape=[
            jax.ShapeDtypeStruct((1, 6, here, CLUSTER), f32),
            jax.ShapeDtypeStruct(pair_list.shape, jnp.int32),
            jax.ShapeDtypeStruct((2,), jnp.int32),
        ],
        in_specs=[in_scalars, in_scalars, in_scalars, in_vectors],
        out_specs=[in_vectors, in_scalars, in_scalars],
        scratch_shapes=tables(here, here)
        + [square] * 4
        + [pltpu.VMEM((here // BATCH, LANES, BATCH * PADDED, 128), f32)]
        + room,
        compiler_params=pltpu.CompilerParams(vmem_limit_bytes=32 * 2**20),
        cost_estimate=pl.CostEstimate(flops=12 * 10**9, bytes_accessed=10**6, transcendentals=0),
        name="own_terms",
    )(pair_list, pair_count, anchor, owned)


def pair_terms(window, order, bounds, inner):
    blocks, _, here, _ = window.shape
    clusters = blocks * here
    sums = pltpu.VMEM((2, LANES, BATCH * PADDED, 128), f32)
    return pl.pallas_call(
        functools.partial(pair_kernel, REACH * here if inner else 0, inner),
        out_shape=jax.ShapeDtypeStruct((blocks, 6, here, CLUSTER), f32),
        in_specs=[in_scalars, in_scalars, in_vectors],
        out_specs=in_vectors,
        scratch_shapes=tables(clusters, here) + [square] * 8 + [sums] * 2 + room * 2,
        compiler_params=pltpu.CompilerParams(vmem_limit_bytes=50 * 2**20),
        cost_estimate=pl.CostEstimate(
            flops=(16 if inner else 150) * 10**9, bytes_accessed=10**6, transcendentals=0
        ),
        name="inner_pairs" if inner else "outer_pairs",
    )(order, bounds, window)


def shards(particles, pair_list, pair_count):
    width = particles.shape[1]
    here = width // CLUSTER
    owned = particles.reshape(7, here, CLUSTER)
    axis = ("gx", "gy")
    others = list(range(-REACH, 0)) + list(range(1, REACH + 1))
    around = {0: owned}
    for offset in others:
        around[offset] = passed_along(owned, axis, -offset)
    anchor = ((lax.axis_index(axis) - REACH) * here).astype(jnp.int32).reshape(1)
    alone, order, bounds = own_terms(owned[None], pair_list, pair_count, anchor)
    window = jnp.stack([around[offset] for offset in range(-REACH, REACH + 1)])
    pieces = pair_terms(window, order, bounds, False)
    inner = pair_terms(owned[None], order, bounds, True)
    result = alone[0] + inner[0] + pieces[REACH]
    for offset in others:
        result = result + passed_along(pieces[offset + REACH], axis, offset)
    final = result.reshape(6, width)
    return (final[:3], final[3:])


def solution(mesh):
    placed = (P(None, ("gx", "gy")), P(("gx", "gy"), None), P(("gx", "gy")))
    return jax.shard_map(
        shards,
        mesh=mesh,
        in_specs=placed,
        out_specs=(P(None, ("gx", "gy")), P(None, ("gx", "gy"))),
        check_vma=False,
    )
```

```python
import functools

import jax
import jax.numpy as jnp
from jax import lax
from jax.experimental import pallas as pl
from jax.experimental.pallas import tpu as pltpu
from jax.sharding import PartitionSpec as P

CLUSTER = 512
REACH = 3
BATCH = 8
ROWS = 8
SUMS = 27
STRIP = 256
LATE = 24
PADDED = 32
PITCH = 40
LANES = CLUSTER // 128
inv_four_pi = 0.07957747154594767
f32 = jnp.float32
bf16 = jnp.bfloat16


def passed_along(value, axis, steps):
    count = lax.axis_size(axis)
    first, last = (max(0, -steps), min(count, count - steps))
    return lax.ppermute(value, axis, [(source, source + steps) for source in range(first, last)])


def cross_list(left, right):
    return [
        left[1] * right[2] - left[2] * right[1],
        left[2] * right[0] - left[0] * right[2],
        left[0] * right[1] - left[1] * right[0],
    ]


def aligned(index, size):
    return pl.ds(pl.multiple_of(index * size, size), size)


def pitched(slot):
    return pl.ds(pl.multiple_of(slot * PITCH, 8), PADDED)


def wide(ref, rows):
    return jnp.concatenate([ref[lane, rows, :] for lane in range(LANES)], axis=1)


def put(ref, rows, value, *lead):
    for lane in range(LANES):
        ref[(*lead, lane, rows, slice(None))] = value[:, lane * 128 : lane * 128 + 128]


def prepare(window, shrink, block, here, table, centres, moments, sources):
    x = [shrink * window[block, c] for c in range(3)]
    a = [window[block, 3 + c] for c in range(3)]
    core = shrink * window[block, 6]
    half = 0.5 * core * core
    middle = [jnp.mean(x[c], axis=1, keepdims=True) for c in range(3)]
    y = [x[c] - middle[c] for c in range(3)]
    first = block * here * ROWS
    for k, plane in enumerate([x[0], x[1], x[2], half, a[0], a[1], a[2], jnp.zeros_like(half)]):
        put(table, pl.ds(first + k, here, stride=ROWS), plane)
    for k in range(3):
        centres[pl.ds(first + k, here, stride=ROWS), :] = jnp.broadcast_to(middle[k], (here, 128))
    b = cross_list(y, a)
    size = y[0] * y[0] + y[1] * y[1] + y[2] * y[2] + half
    planes = a + [y[d] * a[c] for d in range(3) for c in range(3)]
    planes += [y[d] * b[c] for d in range(3) for c in range(3)]
    planes += [size * a[c] for c in range(3)] + [size * b[c] for c in range(3)]
    for k, plane in enumerate(planes):
        put(moments, pl.ds(k, here, stride=PADDED), plane)

    def split(turn, _):
        for index in [turn * 4 + k for k in range(4)]:
            whole = wide(moments, aligned(index, PADDED))
            for part in range(3):
                piece = whole.astype(bf16)
                sources[block * here + index, part * PADDED : (part + 1) * PADDED, :] = piece
                whole = whole - piece.astype(f32)
        return 0

    lax.fori_loop(0, here // 4, split, 0)


def parted(rows):
    high = rows.astype(bf16).astype(f32)
    rest = rows - high
    middle = rest.astype(bf16).astype(f32)
    return high, middle, rest - middle


def features(rows, middle, left):
    place = lax.broadcasted_iota(jnp.int32, rows.shape, 0)
    moved = rows - jnp.concatenate([middle] * LANES, axis=1)
    size = jnp.where(place < 3, moved * moved, jnp.where(place == 3, moved, 0.0))
    size = jnp.sum(size, axis=0, keepdims=True)
    if left:
        whole = jnp.where(place < 3, moved, jnp.where(place == 3, size, jnp.where(place == 4, 1.0, 0.0)))
        h, m, l = parted(whole)
        return jnp.concatenate([h, h, m, m, h, l], axis=0)
    whole = jnp.where(place < 3, -2.0 * moved, jnp.where(place == 3, 1.0, jnp.where(place == 4, size, 0.0)))
    h, m, l = parted(whole)
    return jnp.concatenate([h, m, h, m, l, h], axis=0)


def steepness(target, source, table, centres, high, low, high_across=None, low_across=None):
    step = STRIP
    second = wide(table, aligned(source, ROWS))
    middle = centres[aligned(target, ROWS), :]
    left = features(wide(table, aligned(target, ROWS)), middle, True).astype(bf16).T
    right = features(second, middle, False).astype(bf16)
    for row in range(0, CLUSTER, step):
        rho = jnp.maximum(matmul(left[row : row + step], right), second[3:4, :])
        inverse = lax.rsqrt(rho)
        square = inverse * inverse
        steep = square * square * inverse
        if high_across is None:
            rows = lax.broadcasted_iota(jnp.int32, rho.shape, 0) + row
            steep = jnp.where(rows == lax.broadcasted_iota(jnp.int32, rho.shape, 1), 0.0, steep)
        piece = steep.astype(bf16)
        rest = (steep - piece.astype(f32)).astype(bf16)
        high[row : row + step, :] = piece
        low[row : row + step, :] = rest
        if high_across is not None:
            high_across[:, row : row + step] = piece.T
            low_across[:, row : row + step] = rest.T


def matmul(left, right):
    return lax.dot_general(left, right, (((1,), (0,)), ((), ())), preferred_element_type=f32)


def folded(source, high, low):
    total = matmul(source, high) + matmul(source, low)
    return total[:PADDED] + total[PADDED : 2 * PADDED] + total[2 * PADDED :]


def combine(sums, parity, lane, targets, middles, answers):
    g = [sums[parity, lane, pl.ds(k, BATCH, stride=PITCH), :] for k in range(SUMS)]
    t = [targets[pl.ds(k, BATCH, stride=ROWS), :] for k in (0, 1, 2, 4, 5, 6, 3)]
    x = [t[c] - middles[pl.ds(c, BATCH, stride=ROWS), :] for c in range(3)]
    a = t[3:6]
    plain = g[0:3]
    ya = [g[3 + 3 * d : 6 + 3 * d] for d in range(3)]
    yb = [g[12 + 3 * d : 15 + 3 * d] for d in range(3)]
    b = [ya[1][2] - ya[2][1], ya[2][0] - ya[0][2], ya[0][1] - ya[1][0]]
    size = x[0] * x[0] + x[1] * x[1] + x[2] * x[2] + t[6]
    twice = [2.0 * x[c] for c in range(3)]

    def along(vector, matrix, c):
        return vector[0] * matrix[0][c] + vector[1] * matrix[1][c] + vector[2] * matrix[2][c]

    ka = [size * plain[c] + (g[21 + c] - along(twice, ya, c)) for c in range(3)]
    kb = [size * b[c] + (g[24 + c] - along(twice, yb, c)) for c in range(3)]
    project = a[0] * x[0] + a[1] * x[1] + a[2] * x[2]
    q = [project * plain[c] - along(a, ya, c) for c in range(3)]
    r = [project * b[c] - along(a, yb, c) for c in range(3)]
    turn = cross_list(a, ka)
    moved = cross_list(x, ka)
    tilt = cross_list(x, q)
    for c in range(3):
        answers[pl.ds(c, BATCH, stride=ROWS), :] = -inv_four_pi * (moved[c] - kb[c])
        answers[pl.ds(3 + c, BATCH, stride=ROWS), :] = -inv_four_pi * (
            turn[c] - 3.0 * (tilt[c] - r[c])
        )


def settle(target_of, source_of, live_of, sums, parity, lane, table, centres, total, room):
    targets, middles, answers = room
    for slot in range(BATCH):
        targets[slot * ROWS : (slot + 1) * ROWS, :] = table[lane, aligned(target_of(slot), ROWS), :]
        middles[slot * ROWS : (slot + 1) * ROWS, :] = centres[aligned(source_of(slot), ROWS), :]
    combine(sums, parity, lane, targets, middles, answers)
    for slot in range(BATCH):
        update = answers[slot * ROWS : (slot + 1) * ROWS, :]
        if live_of is not None:
            update = jnp.where(live_of(slot), update, 0.0)
        total[lane, aligned(target_of(slot), ROWS), :] += update


def shrinking(window):
    blocks = window.shape[0]
    largest = jnp.abs(window[0, 0])
    for block in range(blocks):
        for c in range(3):
            largest = jnp.maximum(largest, jnp.abs(window[block, c]))
    largest = jnp.max(jnp.max(largest, axis=0, keepdims=True), axis=1, keepdims=True)
    return 1.0 / jnp.maximum(1.0, 1e-4 * largest)


def begin(window, table, centres, moments, sources, total):
    blocks, _, here, _ = window.shape
    moments[...] = jnp.zeros_like(moments)
    centres[...] = jnp.zeros_like(centres)
    total[...] = jnp.zeros_like(total)
    shrink = shrinking(window)
    for block in range(blocks):
        prepare(window, shrink, block, here, table, centres, moments, sources)


def finish(total, window, out):
    blocks, _, here, _ = out.shape
    shrink = shrinking(window)
    for block in range(blocks):
        for k in range(6):
            whole = wide(total, pl.ds(block * here * ROWS + k, here, stride=ROWS))
            out[block, k] = (shrink * shrink * whole) if k < 3 else (shrink * shrink * shrink * whole)


def own_kernel(
    pairs, count, start, window, out, order, bounds,
    table, centres, moments, sources, total, high0, low0, high1, low1, sums, targets, middles, answers,
):
    here = window.shape[2]
    live = count[0]
    anchor = start[0]
    last = (2 * REACH + 1) * here - 1

    def place(slot, front):
        first = jnp.clip(pairs[slot, 0] - anchor, 0, last)
        second = jnp.clip(pairs[slot, 1] - anchor, 0, last)
        inner = jnp.logical_and(first >= REACH * here, second < (REACH + 1) * here)
        inner = jnp.logical_and(inner, jnp.logical_and(second >= REACH * here, first < (REACH + 1) * here))
        inner = jnp.logical_and(inner, slot - front < LATE)
        where = jnp.where(inner, live - 1 - (slot - front), front)
        order[where, 0] = first
        order[where, 1] = second
        return front + jnp.where(inner, 0, 1)

    bounds[0] = lax.fori_loop(0, live, place, 0)
    bounds[1] = live
    begin(window, table, centres, moments, sources, total)
    answers[...] = jnp.zeros_like(answers)
    high, low = (high0, high1), (low0, low1)
    steepness(0, 0, table, centres, high0, low0)

    def own_turn(turn, _):
        for h in range(2):
            cluster = turn * 2 + h
            following = jnp.minimum(cluster + 1, here - 1)
            steepness(following, following, table, centres, high[1 - h], low[1 - h])
            answer = folded(sources[cluster], high[h][...], low[h][...])
            put(sums, pitched(lax.rem(cluster, BATCH)), answer, lax.div(cluster, BATCH))
        return 0

    lax.fori_loop(0, here // 2, own_turn, 0)

    def own_settle(batch, _):
        own = lambda slot: batch * BATCH + slot
        for lane in range(LANES):
            settle(own, own, None, sums, batch, lane, table, centres, total, (targets, middles, answers))
        return 0

    lax.fori_loop(0, here // BATCH, own_settle, 0)
    finish(total, window, out)


def pair_kernel(
    shift, inner, order, bounds, window, out,
    table, centres, moments, sources, total, high0, low0, high1, low1,
    high_across0, low_across0, high_across1, low_across1, sums_first, sums_second, *rooms,
):
    blocks, _, here, _ = window.shape
    begin(window, table, centres, moments, sources, total)
    room_first, room_second = rooms[:3], rooms[3:]
    for room in (room_first, room_second):
        room[2][...] = jnp.zeros_like(room[2])
    for square in (high1, low1, high_across1, low_across1):
        square[...] = jnp.zeros_like(square)
    squares = (
        (high0, low0, high_across0, low_across0),
        (high1, low1, high_across1, low_across1),
    )
    first_unit = bounds[0] if inner else 0
    end_unit = bounds[1] if inner else bounds[0]

    def chosen(unit, side):
        held = jnp.maximum(jnp.clip(unit, first_unit, end_unit - 1), 0)
        return jnp.clip(order[held, side] - shift, 0, blocks * here - 1)

    def settle_part(turn):
        batch = lax.div(turn, BATCH // 2) - 1
        lane = lax.rem(turn, BATCH // 2)
        parity = lax.rem(batch + 2, 2)
        unit = lambda slot: first_unit + batch * BATCH + slot - 1
        alive = lambda slot: jnp.logical_and(unit(slot) >= first_unit, unit(slot) < end_unit)
        one = lambda slot: chosen(unit(slot), 0)
        two = lambda slot: chosen(unit(slot), 1)
        settle(one, two, alive, sums_first, parity, lane, table, centres, total, room_first)
        settle(two, one, alive, sums_second, parity, lane, table, centres, total, room_second)

    def pair_turn(double, _):
        for half in range(2):
            one_turn(double * 2 + half)
        return 0

    def one_turn(turn):
        base = first_unit + turn * 2
        parity = lax.rem(lax.div(turn, BATCH // 2), 2)
        for h in range(2):
            steepness(chosen(base + h, 0), chosen(base + h, 1), table, centres, *squares[h])
            before = base + h - 1
            rows = pitched(lax.rem(turn, BATCH // 2) * 2 + h)
            hi, lo, hi_across, lo_across = [ref[...] for ref in squares[1 - h]]
            put(sums_second, rows, folded(sources[chosen(before, 0)], hi, lo), parity)
            put(sums_first, rows, folded(sources[chosen(before, 1)], hi_across, lo_across), parity)
        settle_part(turn)

    def settle_turn(turn, _):
        settle_part(turn)
        return 0

    doubles = lax.div(end_unit - first_unit + 4, 4)
    turns = 2 * doubles
    lax.fori_loop(0, doubles, pair_turn, 0)
    quarter = BATCH // 2
    lax.fori_loop(turns, lax.div(turns + quarter - 1, quarter) * quarter + quarter, settle_turn, 0)
    finish(total, window, out)


def tables(clusters, here):
    return [
        pltpu.VMEM((LANES, clusters * ROWS, 128), f32),
        pltpu.VMEM((clusters * ROWS, 128), f32),
        pltpu.VMEM((LANES, here * PADDED, 128), f32),
        pltpu.VMEM((clusters, 3 * PADDED, CLUSTER), bf16),
        pltpu.VMEM((LANES, clusters * ROWS, 128), f32),
    ]


in_scalars = pl.BlockSpec(memory_space=pltpu.SMEM)
in_vectors = pl.BlockSpec(memory_space=pltpu.VMEM)
square = pltpu.VMEM((CLUSTER, CLUSTER), bf16)
room = [pltpu.VMEM((BATCH * ROWS, 128), f32)] * 3


def own_terms(owned, pair_list, pair_count, anchor):
    here = owned.shape[2]
    return pl.pallas_call(
        own_kernel,
        out_shape=[
            jax.ShapeDtypeStruct((1, 6, here, CLUSTER), f32),
            jax.ShapeDtypeStruct(pair_list.shape, jnp.int32),
            jax.ShapeDtypeStruct((2,), jnp.int32),
        ],
        in_specs=[in_scalars, in_scalars, in_scalars, in_vectors],
        out_specs=[in_vectors, in_scalars, in_scalars],
        scratch_shapes=tables(here, here)
        + [square] * 4
        + [pltpu.VMEM((here // BATCH, LANES, BATCH * PITCH, 128), f32)]
        + room,
        compiler_params=pltpu.CompilerParams(vmem_limit_bytes=32 * 2**20),
        cost_estimate=pl.CostEstimate(flops=12 * 10**9, bytes_accessed=10**6, transcendentals=0),
        name="own_terms",
    )(pair_list, pair_count, anchor, owned)


def pair_terms(window, order, bounds, inner):
    blocks, _, here, _ = window.shape
    clusters = blocks * here
    sums = pltpu.VMEM((2, LANES, BATCH * PITCH, 128), f32)
    return pl.pallas_call(
        functools.partial(pair_kernel, REACH * here if inner else 0, inner),
        out_shape=jax.ShapeDtypeStruct((blocks, 6, here, CLUSTER), f32),
        in_specs=[in_scalars, in_scalars, in_vectors],
        out_specs=in_vectors,
        scratch_shapes=tables(clusters, here) + [square] * 8 + [sums] * 2 + room * 2,
        compiler_params=pltpu.CompilerParams(vmem_limit_bytes=50 * 2**20),
        cost_estimate=pl.CostEstimate(
            flops=(16 if inner else 150) * 10**9, bytes_accessed=10**6, transcendentals=0
        ),
        name="inner_pairs" if inner else "outer_pairs",
    )(order, bounds, window)


def shards(particles, pair_list, pair_count):
    width = particles.shape[1]
    here = width // CLUSTER
    owned = particles.reshape(7, here, CLUSTER)
    axis = ("gx", "gy")
    others = list(range(-REACH, 0)) + list(range(1, REACH + 1))
    around = {0: owned}
    for offset in others:
        around[offset] = passed_along(owned, axis, -offset)
    anchor = ((lax.axis_index(axis) - REACH) * here).astype(jnp.int32).reshape(1)
    alone, order, bounds = own_terms(owned[None], pair_list, pair_count, anchor)
    window = jnp.stack([around[offset] for offset in range(-REACH, REACH + 1)])
    pieces = pair_terms(window, order, bounds, False)
    inner = pair_terms(owned[None], order, bounds, True)
    result = alone[0] + inner[0] + pieces[REACH]
    for offset in others:
        result = result + passed_along(pieces[offset + REACH], axis, offset)
    final = result.reshape(6, width)
    return (final[:3], final[3:])


def solution(mesh):
    placed = (P(None, ("gx", "gy")), P(("gx", "gy"), None), P(("gx", "gy")))
    return jax.shard_map(
        shards,
        mesh=mesh,
        in_specs=placed,
        out_specs=(P(None, ("gx", "gy")), P(None, ("gx", "gy"))),
        check_vma=False,
    )
```

```python
import functools

import jax
import jax.numpy as jnp
from jax import lax
from jax.experimental import pallas as pl
from jax.experimental.pallas import tpu as pltpu
from jax.sharding import PartitionSpec as P

CLUSTER = 512
REACH = 3
BATCH = 8
ROWS = 8
SUMS = 27
STRIP = 256
LATE = 24
LEAST = 8
PADDED = 32
PITCH = 40
LANES = CLUSTER // 128
inv_four_pi = 0.07957747154594767
f32 = jnp.float32
bf16 = jnp.bfloat16


def passed_along(value, axis, steps):
    count = lax.axis_size(axis)
    first, last = (max(0, -steps), min(count, count - steps))
    return lax.ppermute(value, axis, [(source, source + steps) for source in range(first, last)])


def cross_list(left, right):
    return [
        left[1] * right[2] - left[2] * right[1],
        left[2] * right[0] - left[0] * right[2],
        left[0] * right[1] - left[1] * right[0],
    ]


def aligned(index, size):
    return pl.ds(pl.multiple_of(index * size, size), size)


def pitched(slot):
    return pl.ds(pl.multiple_of(slot * PITCH, 8), PADDED)


def wide(ref, rows):
    return jnp.concatenate([ref[lane, rows, :] for lane in range(LANES)], axis=1)


def put(ref, rows, value, *lead):
    for lane in range(LANES):
        ref[(*lead, lane, rows, slice(None))] = value[:, lane * 128 : lane * 128 + 128]


def prepare(window, shrink, block, here, table, centres, moments, sources):
    x = [shrink * window[block, c] for c in range(3)]
    a = [window[block, 3 + c] for c in range(3)]
    core = shrink * window[block, 6]
    half = 0.5 * core * core
    middle = [jnp.mean(x[c], axis=1, keepdims=True) for c in range(3)]
    y = [x[c] - middle[c] for c in range(3)]
    first = block * here * ROWS
    for k, plane in enumerate([x[0], x[1], x[2], half, a[0], a[1], a[2], jnp.zeros_like(half)]):
        put(table, pl.ds(first + k, here, stride=ROWS), plane)
    for k in range(3):
        centres[pl.ds(first + k, here, stride=ROWS), :] = jnp.broadcast_to(middle[k], (here, 128))
    b = cross_list(y, a)
    size = y[0] * y[0] + y[1] * y[1] + y[2] * y[2] + half
    planes = a + [y[d] * a[c] for d in range(3) for c in range(3)]
    planes += [y[d] * b[c] for d in range(3) for c in range(3)]
    planes += [size * a[c] for c in range(3)] + [size * b[c] for c in range(3)]
    for k, plane in enumerate(planes):
        put(moments, pl.ds(k, here, stride=PADDED), plane)

    def split(turn, _):
        for index in [turn * 4 + k for k in range(4)]:
            whole = wide(moments, aligned(index, PADDED))
            for part in range(3):
                piece = whole.astype(bf16)
                sources[block * here + index, part * PADDED : (part + 1) * PADDED, :] = piece
                whole = whole - piece.astype(f32)
        return 0

    lax.fori_loop(0, here // 4, split, 0)


def parted(rows):
    high = rows.astype(bf16).astype(f32)
    rest = rows - high
    middle = rest.astype(bf16).astype(f32)
    return high, middle, rest - middle


def features(rows, middle, left):
    place = lax.broadcasted_iota(jnp.int32, rows.shape, 0)
    moved = rows - jnp.concatenate([middle] * LANES, axis=1)
    size = jnp.where(place < 3, moved * moved, jnp.where(place == 3, moved, 0.0))
    size = jnp.sum(size, axis=0, keepdims=True)
    if left:
        whole = jnp.where(place < 3, moved, jnp.where(place == 3, size, jnp.where(place == 4, 1.0, 0.0)))
        h, m, l = parted(whole)
        return jnp.concatenate([h, h, m, m, h, l], axis=0)
    whole = jnp.where(place < 3, -2.0 * moved, jnp.where(place == 3, 1.0, jnp.where(place == 4, size, 0.0)))
    h, m, l = parted(whole)
    return jnp.concatenate([h, m, h, m, l, h], axis=0)


def steepness(target, source, table, centres, high, low, high_across=None, low_across=None):
    step = STRIP
    second = wide(table, aligned(source, ROWS))
    middle = centres[aligned(target, ROWS), :]
    left = features(wide(table, aligned(target, ROWS)), middle, True).astype(bf16).T
    right = features(second, middle, False).astype(bf16)
    for row in range(0, CLUSTER, step):
        rho = jnp.maximum(matmul(left[row : row + step], right), second[3:4, :])
        inverse = lax.rsqrt(rho)
        square = inverse * inverse
        steep = square * square * inverse
        if high_across is None:
            rows = lax.broadcasted_iota(jnp.int32, rho.shape, 0) + row
            steep = jnp.where(rows == lax.broadcasted_iota(jnp.int32, rho.shape, 1), 0.0, steep)
        piece = steep.astype(bf16)
        rest = (steep - piece.astype(f32)).astype(bf16)
        high[row : row + step, :] = piece
        low[row : row + step, :] = rest
        if high_across is not None:
            high_across[:, row : row + step] = piece.T
            low_across[:, row : row + step] = rest.T


def matmul(left, right):
    return lax.dot_general(left, right, (((1,), (0,)), ((), ())), preferred_element_type=f32)


def folded(source, high, low):
    total = matmul(source, high) + matmul(source, low)
    return total[:PADDED] + total[PADDED : 2 * PADDED] + total[2 * PADDED :]


def combine(sums, parity, lane, targets, middles, answers):
    g = [sums[parity, lane, pl.ds(k, BATCH, stride=PITCH), :] for k in range(SUMS)]
    t = [targets[pl.ds(k, BATCH, stride=ROWS), :] for k in (0, 1, 2, 4, 5, 6, 3)]
    x = [t[c] - middles[pl.ds(c, BATCH, stride=ROWS), :] for c in range(3)]
    a = t[3:6]
    plain = g[0:3]
    ya = [g[3 + 3 * d : 6 + 3 * d] for d in range(3)]
    yb = [g[12 + 3 * d : 15 + 3 * d] for d in range(3)]
    b = [ya[1][2] - ya[2][1], ya[2][0] - ya[0][2], ya[0][1] - ya[1][0]]
    size = x[0] * x[0] + x[1] * x[1] + x[2] * x[2] + t[6]
    twice = [2.0 * x[c] for c in range(3)]

    def along(vector, matrix, c):
        return vector[0] * matrix[0][c] + vector[1] * matrix[1][c] + vector[2] * matrix[2][c]

    ka = [size * plain[c] + (g[21 + c] - along(twice, ya, c)) for c in range(3)]
    kb = [size * b[c] + (g[24 + c] - along(twice, yb, c)) for c in range(3)]
    project = a[0] * x[0] + a[1] * x[1] + a[2] * x[2]
    q = [project * plain[c] - along(a, ya, c) for c in range(3)]
    r = [project * b[c] - along(a, yb, c) for c in range(3)]
    turn = cross_list(a, ka)
    moved = cross_list(x, ka)
    tilt = cross_list(x, q)
    for c in range(3):
        answers[pl.ds(c, BATCH, stride=ROWS), :] = -inv_four_pi * (moved[c] - kb[c])
        answers[pl.ds(3 + c, BATCH, stride=ROWS), :] = -inv_four_pi * (
            turn[c] - 3.0 * (tilt[c] - r[c])
        )


def settle(target_of, source_of, live_of, sums, parity, lane, table, centres, total, room):
    targets, middles, answers = room
    for slot in range(BATCH):
        targets[slot * ROWS : (slot + 1) * ROWS, :] = table[lane, aligned(target_of(slot), ROWS), :]
        middles[slot * ROWS : (slot + 1) * ROWS, :] = centres[aligned(source_of(slot), ROWS), :]
    combine(sums, parity, lane, targets, middles, answers)
    for slot in range(BATCH):
        update = answers[slot * ROWS : (slot + 1) * ROWS, :]
        if live_of is not None:
            update = jnp.where(live_of(slot), update, 0.0)
        total[lane, aligned(target_of(slot), ROWS), :] += update


def shrinking(window):
    blocks = window.shape[0]
    largest = jnp.abs(window[0, 0])
    for block in range(blocks):
        for c in range(3):
            largest = jnp.maximum(largest, jnp.abs(window[block, c]))
    largest = jnp.max(jnp.max(largest, axis=0, keepdims=True), axis=1, keepdims=True)
    return 1.0 / jnp.maximum(1.0, 1e-4 * largest)


def begin(window, table, centres, moments, sources, total):
    blocks, _, here, _ = window.shape
    moments[...] = jnp.zeros_like(moments)
    centres[...] = jnp.zeros_like(centres)
    total[...] = jnp.zeros_like(total)
    shrink = shrinking(window)
    for block in range(blocks):
        prepare(window, shrink, block, here, table, centres, moments, sources)


def finish(total, window, out):
    blocks, _, here, _ = out.shape
    shrink = shrinking(window)
    for block in range(blocks):
        for k in range(6):
            whole = wide(total, pl.ds(block * here * ROWS + k, here, stride=ROWS))
            out[block, k] = (shrink * shrink * whole) if k < 3 else (shrink * shrink * shrink * whole)


def own_kernel(
    pairs, count, start, window, out, order, bounds,
    table, centres, moments, sources, total, high0, low0, high1, low1, sums, targets, middles, answers,
):
    here = window.shape[2]
    live = count[0]
    anchor = start[0]
    last = (2 * REACH + 1) * here - 1
    late = jnp.clip(LATE + live - pairs.shape[0], LEAST, LATE)

    def place(slot, front):
        first = jnp.clip(pairs[slot, 0] - anchor, 0, last)
        second = jnp.clip(pairs[slot, 1] - anchor, 0, last)
        inner = jnp.logical_and(first >= REACH * here, second < (REACH + 1) * here)
        inner = jnp.logical_and(inner, jnp.logical_and(second >= REACH * here, first < (REACH + 1) * here))
        inner = jnp.logical_and(inner, slot - front < late)
        where = jnp.where(inner, live - 1 - (slot - front), front)
        order[where, 0] = first
        order[where, 1] = second
        return front + jnp.where(inner, 0, 1)

    bounds[0] = lax.fori_loop(0, live, place, 0)
    bounds[1] = live
    begin(window, table, centres, moments, sources, total)
    answers[...] = jnp.zeros_like(answers)
    high, low = (high0, high1), (low0, low1)
    steepness(0, 0, table, centres, high0, low0)

    def own_turn(turn, _):
        for h in range(2):
            cluster = turn * 2 + h
            following = jnp.minimum(cluster + 1, here - 1)
            steepness(following, following, table, centres, high[1 - h], low[1 - h])
            answer = folded(sources[cluster], high[h][...], low[h][...])
            put(sums, pitched(lax.rem(cluster, BATCH)), answer, lax.div(cluster, BATCH))
        return 0

    lax.fori_loop(0, here // 2, own_turn, 0)

    def own_settle(batch, _):
        own = lambda slot: batch * BATCH + slot
        for lane in range(LANES):
            settle(own, own, None, sums, batch, lane, table, centres, total, (targets, middles, answers))
        return 0

    lax.fori_loop(0, here // BATCH, own_settle, 0)
    finish(total, window, out)


def pair_kernel(
    shift, inner, order, bounds, window, out,
    table, centres, moments, sources, total, high0, low0, high1, low1,
    high_across0, low_across0, high_across1, low_across1, sums_first, sums_second, *rooms,
):
    blocks, _, here, _ = window.shape
    begin(window, table, centres, moments, sources, total)
    room_first, room_second = rooms[:3], rooms[3:]
    for room in (room_first, room_second):
        room[2][...] = jnp.zeros_like(room[2])
    for square in (high1, low1, high_across1, low_across1):
        square[...] = jnp.zeros_like(square)
    squares = (
        (high0, low0, high_across0, low_across0),
        (high1, low1, high_across1, low_across1),
    )
    first_unit = bounds[0] if inner else 0
    end_unit = bounds[1] if inner else bounds[0]

    def chosen(unit, side):
        held = jnp.maximum(jnp.clip(unit, first_unit, end_unit - 1), 0)
        return jnp.clip(order[held, side] - shift, 0, blocks * here - 1)

    def settle_part(turn):
        batch = lax.div(turn, BATCH // 2) - 1
        lane = lax.rem(turn, BATCH // 2)
        parity = lax.rem(batch + 2, 2)
        unit = lambda slot: first_unit + batch * BATCH + slot - 1
        alive = lambda slot: jnp.logical_and(unit(slot) >= first_unit, unit(slot) < end_unit)
        one = lambda slot: chosen(unit(slot), 0)
        two = lambda slot: chosen(unit(slot), 1)
        settle(one, two, alive, sums_first, parity, lane, table, centres, total, room_first)
        settle(two, one, alive, sums_second, parity, lane, table, centres, total, room_second)

    def pair_turn(double, _):
        for half in range(2):
            one_turn(double * 2 + half)
        return 0

    def one_turn(turn):
        base = first_unit + turn * 2
        parity = lax.rem(lax.div(turn, BATCH // 2), 2)
        for h in range(2):
            steepness(chosen(base + h, 0), chosen(base + h, 1), table, centres, *squares[h])
            before = base + h - 1
            rows = pitched(lax.rem(turn, BATCH // 2) * 2 + h)
            hi, lo, hi_across, lo_across = [ref[...] for ref in squares[1 - h]]
            put(sums_second, rows, folded(sources[chosen(before, 0)], hi, lo), parity)
            put(sums_first, rows, folded(sources[chosen(before, 1)], hi_across, lo_across), parity)
        settle_part(turn)

    def settle_turn(turn, _):
        settle_part(turn)
        return 0

    doubles = lax.div(end_unit - first_unit + 4, 4)
    turns = 2 * doubles
    lax.fori_loop(0, doubles, pair_turn, 0)
    quarter = BATCH // 2
    lax.fori_loop(turns, lax.div(turns + quarter - 1, quarter) * quarter + quarter, settle_turn, 0)
    finish(total, window, out)


def tables(clusters, here):
    return [
        pltpu.VMEM((LANES, clusters * ROWS, 128), f32),
        pltpu.VMEM((clusters * ROWS, 128), f32),
        pltpu.VMEM((LANES, here * PADDED, 128), f32),
        pltpu.VMEM((clusters, 3 * PADDED, CLUSTER), bf16),
        pltpu.VMEM((LANES, clusters * ROWS, 128), f32),
    ]


in_scalars = pl.BlockSpec(memory_space=pltpu.SMEM)
in_vectors = pl.BlockSpec(memory_space=pltpu.VMEM)
square = pltpu.VMEM((CLUSTER, CLUSTER), bf16)
room = [pltpu.VMEM((BATCH * ROWS, 128), f32)] * 3


def own_terms(owned, pair_list, pair_count, anchor):
    here = owned.shape[2]
    return pl.pallas_call(
        own_kernel,
        out_shape=[
            jax.ShapeDtypeStruct((1, 6, here, CLUSTER), f32),
            jax.ShapeDtypeStruct(pair_list.shape, jnp.int32),
            jax.ShapeDtypeStruct((2,), jnp.int32),
        ],
        in_specs=[in_scalars, in_scalars, in_scalars, in_vectors],
        out_specs=[in_vectors, in_scalars, in_scalars],
        scratch_shapes=tables(here, here)
        + [square] * 4
        + [pltpu.VMEM((here // BATCH, LANES, BATCH * PITCH, 128), f32)]
        + room,
        compiler_params=pltpu.CompilerParams(vmem_limit_bytes=32 * 2**20),
        cost_estimate=pl.CostEstimate(flops=12 * 10**9, bytes_accessed=10**6, transcendentals=0),
        name="own_terms",
    )(pair_list, pair_count, anchor, owned)


def pair_terms(window, order, bounds, inner):
    blocks, _, here, _ = window.shape
    clusters = blocks * here
    sums = pltpu.VMEM((2, LANES, BATCH * PITCH, 128), f32)
    return pl.pallas_call(
        functools.partial(pair_kernel, REACH * here if inner else 0, inner),
        out_shape=jax.ShapeDtypeStruct((blocks, 6, here, CLUSTER), f32),
        in_specs=[in_scalars, in_scalars, in_vectors],
        out_specs=in_vectors,
        scratch_shapes=tables(clusters, here) + [square] * 8 + [sums] * 2 + room * 2,
        compiler_params=pltpu.CompilerParams(vmem_limit_bytes=50 * 2**20),
        cost_estimate=pl.CostEstimate(
            flops=(16 if inner else 150) * 10**9, bytes_accessed=10**6, transcendentals=0
        ),
        name="inner_pairs" if inner else "outer_pairs",
    )(order, bounds, window)


def shards(particles, pair_list, pair_count):
    width = particles.shape[1]
    here = width // CLUSTER
    owned = particles.reshape(7, here, CLUSTER)
    axis = ("gx", "gy")
    others = list(range(-REACH, 0)) + list(range(1, REACH + 1))
    around = {0: owned}
    for offset in others:
        around[offset] = passed_along(owned, axis, -offset)
    anchor = ((lax.axis_index(axis) - REACH) * here).astype(jnp.int32).reshape(1)
    alone, order, bounds = own_terms(owned[None], pair_list, pair_count, anchor)
    window = jnp.stack([around[offset] for offset in range(-REACH, REACH + 1)])
    pieces = pair_terms(window, order, bounds, False)
    inner = pair_terms(owned[None], order, bounds, True)
    result = alone[0] + inner[0] + pieces[REACH]
    for offset in others:
        result = result + passed_along(pieces[offset + REACH], axis, offset)
    final = result.reshape(6, width)
    return (final[:3], final[3:])


def solution(mesh):
    placed = (P(None, ("gx", "gy")), P(("gx", "gy"), None), P(("gx", "gy")))
    return jax.shard_map(
        shards,
        mesh=mesh,
        in_specs=placed,
        out_specs=(P(None, ("gx", "gy")), P(None, ("gx", "gy"))),
        check_vma=False,
    )
```
